32 devices in a mesh: path: 8 (over z, y), tile: 4 (over x, core).
Axes of the slice: x: 2, y: 2, z: 4, core: 2. Of those that a mesh axis runs over, the one named last changes fastest.
Arguments:
- state0: float32 [3, 8, 64, 4096], P(None, 'path', 'tile'), may hold values from -6 to 6
- intensity: float32 [8, 64, 4096], P('path', 'tile'), may hold values from -4 to 4
- absorption: float32 [64, 4096], P('tile', 'path'), may hold values from 0.5 to 2
- screen_adjoint: float32 [64, 4096], P('tile', 'path'), may hold values from -6 to 6
Outputs:
- state_adjoint: float32 [3, 8, 64, 4096], P(None, 'path', 'tile')
- absorption_grad: float32 [64, 4096], P('tile', 'path')
The draws below stay inside these ranges and needn't reach their ends.
All inputs are finite; a program needn't handle non-finite values.
Results may differ from the reference program's by a relative error of at most 0.00002.
Values sent between devices are 32-bit elements; how exact they have to be, the bound alone decides.
A program may use at most 64 MiB of HBM per device.

```python
import math
import jax
import jax.numpy as jnp
from jax import lax

NY = 4096
STEPS = 8
PLANES = 8
NX = 64


def with_spikes(result, rng, source, target, parts, factor):
    owner, partner = [(jnp.arange(result.shape[dim]) // (result.shape[dim] // parts)).reshape([-1 if axis == dim else 1 for axis in range(result.ndim)]) for dim in (source, target)]
    chosen = jax.random.permutation(rng, parts)[partner]
    strong = (owner == chosen) | (owner == (partner + parts // 2) % parts)
    return jnp.where(strong, factor * result, result)


def block_scale(stream_key, shape, cuts, smallest, largest):
    gain, own = 1.0, jax.random.fold_in(stream_key, 6)
    for position, parts in cuts:
        steps = jnp.exp(jax.random.uniform(jax.random.fold_in(own, position), (parts,), jnp.float32, smallest / len(cuts), largest / len(cuts)))
        gain = gain * jnp.repeat(steps, shape[position] // parts).reshape([-1 if axis == position else 1 for axis in range(len(shape))])
    return gain


def scatter_about(stream_key, shape, deviation, bound, split=(), kind=jnp.bfloat16):
    values = jax.random.normal(stream_key, shape, jnp.float32) * deviation
    if len(split) > 0:
        values = block_scale(stream_key, shape, split, -0.22, 0.18) * values
    return jnp.clip(values, min=-bound, max=bound).astype(kind)


def gaussian_with(rng, shape, scale, limit, split, heavy, kind=jnp.bfloat16):
    values = scale * jax.random.normal(rng, shape, jnp.float32)
    if split:
        values = values * block_scale(rng, shape, split, -0.22, 0.18)
    return jnp.clip(with_spikes(values, jax.random.fold_in(rng, 3), *heavy), -limit, limit).astype(kind)


def setup_inputs(seed: int = 0) -> dict:
    key_of = jax.random.split(jax.random.key(seed), 5)
    state0 = scatter_about(key_of[0], (3, PLANES, NX, NY), 1.0, 6.0, ((1, 8), (2, 4)), jnp.float32)
    intensity = gaussian_with(key_of[1], (PLANES, NX, NY), 1.0, 4.0, ((0, 8), (1, 4)), (0, 2, 8, 2.0), jnp.float32)
    absorption = jnp.clip(jnp.exp(math.log(2.0) - 1.3862944 * jax.random.uniform(key_of[2], (NX, NY), jnp.float32) ** block_scale(key_of[2], (NX, NY), ((0, 4), (1, 8)), -0.2, 0.2)), 0.5, 2.0)
    screen_adjoint = scatter_about(key_of[3], (NX, NY), 1.0, 6.0, ((0, 4), (1, 8)), jnp.float32)
    return {"state0": state0, "intensity": intensity, "absorption": absorption, "screen_adjoint": screen_adjoint}


KAPPA = 0.65
DAMPING = 0.99
HEATING = 0.06
COUPLING = 0.5

def row_after(field):
    return jnp.pad(field[1:], ((0, 1), (0, 0)))

def row_before(field):
    return jnp.pad(field[:-1], ((1, 0), (0, 0)))

def col_after(field):
    return jnp.pad(field[:, 1:], ((0, 0), (0, 1)))

def col_before(field):
    return jnp.pad(field[:, :-1], ((0, 0), (1, 0)))

def window(density, across, along, absorb, light):
    heat = absorb * light
    for step in range(STEPS):
        across = across - KAPPA * (row_after(density) - density)
        along = along - KAPPA * (col_after(density) - density)
        density = DAMPING * density - KAPPA * (across - row_before(across) + along - col_before(along)) + HEATING * heat * (1.0 + COUPLING * density)
    return (density, across, along)

def reference(state0, intensity, absorption, screen_adjoint):
    zeros = jnp.zeros_like(screen_adjoint)

    def one_plane(total, items):
        start, light = items

        def run(density, across, along, absorb):
            return window(density, across, along, absorb, light)
        finals, pull = jax.vjp(run, start[0], start[1], start[2], absorption)
        dual_density, dual_across, dual_along, grad_abs = pull((screen_adjoint, zeros, zeros))
        return (total + grad_abs, jnp.stack([dual_density, dual_across, dual_along]))
    total, duals = lax.scan(one_plane, zeros, (jnp.moveaxis(state0, 1, 0), intensity))
    return (jnp.moveaxis(duals, 0, 1), total)
```

```python
import functools

import jax
import jax.numpy as jnp
from jax import lax
from jax.experimental import pallas as pl
from jax.experimental.pallas import tpu as pltpu
from jax.sharding import PartitionSpec as P

MESH = pl.DeviceIdType.MESH
STEPS = 8
KAPPA = 0.65
DAMPING = 0.99
HEATING = 0.06
COUPLING = 0.5
LANES = 128
SUB = 8
DEPTH = 4
TOP = 2 * SUB
GROUP = 4


def kernel(n, tiles, state, light, absorb, screen, out_state, out_grad,
           xb, yb, wy, maps, beam, ub, vb, stage, total, part, share, done, gsum,
           load_sem, ag_send, ag_recv, hx_send, hx_recv, hq_send, hq_recv, rs_send, rs_recv, out_sem):
    depth = DEPTH if n % DEPTH == 0 else 1
    wide = n // depth
    row_tiles, cols = light.shape[0], light.shape[1]
    rows = row_tiles * SUB
    span = rows + 2 * SUB
    block = cols // n
    me = lax.axis_index("path")
    tile = lax.axis_index("tile")
    my_z, my_y = me // wide, lax.rem(me, wide)
    has_up, has_down = tile > 0, tile < tiles - 1

    loads = []
    for i in range(row_tiles):
        low = pl.ds(i * SUB, SUB)
        own = pl.ds(me * block, block)
        for src, dst in (
            (absorb.at[i], maps.at[0, own, low]),
            (screen.at[i], maps.at[1, own, low]),
            (light.at[i], beam.at[:, low]),
            (state.at[1, i], ub.at[:, low]),
            (state.at[2, i], vb.at[pl.ds(1, cols), low]),
            (state.at[0, i], xb.at[1, pl.ds(1, cols), pl.ds(TOP + i * SUB, SUB)]),
        ):
            loads.append(pltpu.make_async_copy(src, dst, load_sem.at[len(loads)]))
            loads[-1].start()

    barrier = pltpu.get_barrier_semaphore()
    for d in range(1, n):
        pl.semaphore_signal(barrier, inc=1, device_id={"path": lax.rem(me + d, n)}, device_id_type=MESH)

    @pl.when(has_up)
    def _():
        pl.semaphore_signal(barrier, inc=1, device_id={"tile": tile - 1}, device_id_type=MESH)

    @pl.when(has_down)
    def _():
        pl.semaphore_signal(barrier, inc=1, device_id={"tile": tile + 1}, device_id_type=MESH)

    greeted = n - 1 + has_up.astype(jnp.int32) + has_down.astype(jnp.int32)
    pl.semaphore_wait(barrier, greeted)

    def map_copy(owner, target, slot):
        ref = maps.at[:, pl.ds(owner * block, block)]
        return pltpu.make_async_remote_copy(
            src_ref=ref, dst_ref=ref, send_sem=ag_send.at[slot], recv_sem=ag_recv.at[owner],
            device_id={"path": target}, device_id_type=MESH)

    for i in range(row_tiles):
        loads[6 * i].wait()
        loads[6 * i + 1].wait()
    sends = []
    for d in [x for x in (2, 1, 3) if x < depth]:
        sends.append(map_copy(me, lax.rem(my_z + d, depth) * wide + my_y, len(sends)))
        sends[-1].start()
    for d in range(1, wide):
        sends.append(map_copy(me, my_z * wide + lax.rem(my_y + d, wide), len(sends)))
        sends[-1].start()

    blank = jnp.zeros((span, LANES), jnp.float32)
    vb[0] = jnp.zeros((rows, LANES), jnp.float32)
    total[cols] = jnp.zeros((rows + SUB, LANES), jnp.float32)
    for t in range(1, STEPS + 1):
        xb[t, cols + 1, pl.ds(SUB, span)] = blank
        yb[t, cols + 1, pl.ds(SUB, span)] = blank

    @pl.loop(0, cols)
    def _(j):
        wy[j] = blank

    strip = jnp.zeros((2, SUB, LANES), jnp.float32)

    @pl.when(jnp.logical_not(has_up))
    def _():
        @pl.loop(0, cols)
        def _(j):
            xb[pl.ds(0, 2), 1 + j, pl.ds(SUB, SUB)] = strip
            yb[pl.ds(0, 2), 1 + j, pl.ds(SUB, SUB)] = strip

    @pl.when(jnp.logical_not(has_down))
    def _():
        @pl.loop(0, cols)
        def _(j):
            xb[pl.ds(0, 2), 1 + j, pl.ds(TOP + rows, SUB)] = strip
            yb[pl.ds(0, 2), 1 + j, pl.ds(TOP + rows, SUB)] = strip

    for i in range(row_tiles):
        for c in range(2, 6):
            loads[6 * i + c].wait()
    row_of = lax.broadcasted_iota(jnp.int32, (rows, LANES), 0)
    lane_of = lax.broadcasted_iota(jnp.int32, (rows, LANES), 1)

    @pl.loop(0, cols)
    def _(j):
        u, v = ub[j], vb[1 + j]
        before = jnp.where(row_of == 0, 0.0, pltpu.roll(u, 1, 0))
        left = jnp.where(lane_of == 0, pltpu.roll(vb[j], 1, 1), pltpu.roll(v, 1, 1))
        w = KAPPA * ((u - before) + (v - left))
        xb[0, 1 + j, pl.ds(TOP, rows)] = w
        density = xb[1, 1 + j, pl.ds(TOP, rows)]
        stage[0, 0, j] = w[:SUB]
        stage[0, 1, j] = density[:SUB]
        last = KAPPA * pltpu.roll(u[rows - SUB:], 1, 0)
        stage[1, 0, j] = jnp.where(row_of[:SUB] == 0, last, w[rows - SUB:])
        stage[1, 1, j] = density[rows - SUB:]

    def state_copy(way):
        return pltpu.make_async_remote_copy(
            src_ref=stage.at[way],
            dst_ref=xb.at[pl.ds(0, 2), pl.ds(1, cols), pl.ds(TOP + rows if way == 0 else SUB, SUB)],
            send_sem=hx_send.at[way], recv_sem=hx_recv.at[way],
            device_id={"tile": tile - 1 if way == 0 else tile + 1}, device_id_type=MESH)

    def heat_copy(way, owner):
        at = pl.ds(1 + owner * block, block)
        first = TOP if way == 0 else TOP + rows - SUB
        return pltpu.make_async_remote_copy(
            src_ref=yb.at[pl.ds(0, 2), at, pl.ds(first, SUB)],
            dst_ref=yb.at[pl.ds(0, 2), at, pl.ds(TOP + rows if way == 0 else SUB, SUB)],
            send_sem=hq_send.at[way, owner], recv_sem=hq_recv.at[way, owner],
            device_id={"tile": tile - 1 if way == 0 else tile + 1}, device_id_type=MESH)

    @pl.when(has_up)
    def _():
        state_copy(0).start()

    @pl.when(has_down)
    def _():
        state_copy(1).start()

    def use(owner):
        for i in range(block):
            j = owner * block + i
            yb[0, 1 + j, pl.ds(TOP, rows)] = HEATING * (maps[0, j] * beam[j])
            yb[1, 1 + j, pl.ds(TOP, rows)] = maps[1, j]

        @pl.when(has_up)
        def _():
            heat_copy(0, owner).start()

        @pl.when(has_down)
        def _():
            heat_copy(1, owner).start()

    use(me)
    for d in [x for x in (1, 3, 2) if x < depth]:
        owner = lax.rem(my_z + d, depth) * wide + my_y
        map_copy(owner, owner, 0).wait_recv()
        for e in range(1, wide):
            sends.append(map_copy(owner, my_z * wide + lax.rem(my_y + e, wide), len(sends)))
            sends[-1].start()
        use(owner)
    for d in [x for x in (0, 1, 3, 2) if x < depth]:
        for e in range(1, wide):
            owner = lax.rem(my_z + d, depth) * wide + lax.rem(my_y + e, wide)
            map_copy(owner, owner, 0).wait_recv()
            use(owner)

    @pl.when(has_up)
    def _():
        state_copy(1).wait_recv()

        @pl.loop(0, cols)
        def _(j):
            above = jnp.where(row_of[:SUB] == 0, xb[0, 1 + j, pl.ds(SUB, SUB)], 0.0)
            xb[0, 1 + j, pl.ds(TOP, SUB)] = xb[0, 1 + j, pl.ds(TOP, SUB)] - above

    @pl.when(has_down)
    def _():
        state_copy(0).wait_recv()

        @pl.loop(0, cols)
        def _(j):
            last = KAPPA * pltpu.roll(ub[j, pl.ds(rows - SUB, SUB)], 1, 0)
            above = jnp.where(row_of[:SUB] == 0, last, 0.0)
            xb[0, 1 + j, pl.ds(TOP + rows, SUB)] = xb[0, 1 + j, pl.ds(TOP + rows, SUB)] - above

    @pl.when(has_up)
    def _():
        @pl.loop(0, n)
        def _(b):
            heat_copy(1, b).wait_recv()

    @pl.when(has_down)
    def _():
        @pl.loop(0, n)
        def _(b):
            heat_copy(0, b).wait_recv()

    place = tile * rows - SUB + lax.broadcasted_iota(jnp.int32, (span, LANES), 0)
    inside = (place >= 0) & (place < tiles * rows)
    near = jnp.where(inside, KAPPA * KAPPA, 0.0)
    here = jnp.where(place == 0, 3.0, 4.0) * (KAPPA * KAPPA)
    lane = lax.broadcasted_iota(jnp.int32, (span, LANES), 1)

    def pad_left(field, t):
        field[t, 0, pl.ds(SUB, span)] = pltpu.roll(field[t, 1, pl.ds(SUB, span)], LANES - 1, 1)

    pad_left(xb, 1)
    pad_left(yb, 1)

    def spread(field, t, first, count, start, size, near, here, lane):
        window = [field[t, first + i, pl.ds(start, size)] for i in range(count + 2)]
        right = [pltpu.roll(x, 1, 1) for x in window[:-1]]
        left = [pltpu.roll(x, LANES - 1, 1) for x in window[1:]]
        found = []
        for i in range(count):
            before = jnp.where(lane == 0, right[i], right[i + 1])
            after = jnp.where(lane == LANES - 1, left[i + 1], left[i])
            upper = field[t, first + 1 + i, pl.ds(start - 1, size)]
            lower = field[t, first + 1 + i, pl.ds(start + 1, size)]
            x = window[i + 1]
            found.append((x, near * ((before + after) + (upper + lower)) - here * x))
        return found

    @pl.loop(1, STEPS)
    def _(t):
        @pl.loop(0, cols // GROUP)
        def _(g):
            base = g * GROUP
            args = (t, base, GROUP, SUB, span, near, here, lane)
            for i, (x, change) in enumerate(spread(xb, *args)):
                heat = yb[0, base + 1 + i, pl.ds(SUB, span)]
                w = xb[0, base + 1 + i, pl.ds(SUB, span)] - change
                xb[0, base + 1 + i, pl.ds(SUB, span)] = w
                xb[t + 1, base + 1 + i, pl.ds(SUB, span)] = (DAMPING + COUPLING * heat) * x + (heat - w)
            for i, (y, change) in enumerate(spread(yb, *args)):
                heat = yb[0, base + 1 + i, pl.ds(SUB, span)]
                w = wy[base + i] - change
                wy[base + i] = w
                yb[t + 1, base + 1 + i, pl.ds(SUB, span)] = (DAMPING + COUPLING * heat) * y - w

        pad_left(xb, t + 1)
        pad_left(yb, t + 1)

    def grad_copy(owner, slot):
        return pltpu.make_async_remote_copy(
            src_ref=part.at[pl.ds(owner * block, block)], dst_ref=share.at[me],
            send_sem=rs_send.at[slot], recv_sem=rs_recv.at[me],
            device_id={"path": owner}, device_id_type=MESH)

    def gradient(owner):
        @pl.loop(0, block)
        def _(i):
            j = owner * block + i
            both = [yb[1 + t, 1 + j, pl.ds(TOP, rows + SUB)] for t in range(STEPS)]
            add = both[0]
            for t in range(1, STEPS):
                add = add + both[t]
            mix = both[STEPS - 1][:rows] * xb[1, 1 + j, pl.ds(TOP, rows)]
            for t in range(1, STEPS):
                mix = mix + both[STEPS - 1 - t][:rows] * xb[1 + t, 1 + j, pl.ds(TOP, rows)]
            total[j] = add
            part[j] = beam[j] * (HEATING * add[:rows] + (HEATING * COUPLING) * mix)

    @pl.loop(1, n)
    def _(d):
        owner = lax.rem(me + d, n)
        gradient(owner)
        grad_copy(owner, d).start()

    gradient(me)

    inner = slice(SUB, SUB + rows)

    @pl.loop(0, cols // GROUP)
    def _(g):
        base = g * GROUP
        found = spread(yb, STEPS, base, GROUP, TOP, rows, near[inner], here[inner], lane[inner])
        for i, (y, change) in enumerate(found):
            j = base + i
            heat = yb[0, 1 + j, pl.ds(TOP, rows)]
            w = wy[j, pl.ds(SUB, rows)] - change
            final = (DAMPING + COUPLING * heat) * y - w
            add = total[j, pl.ds(0, rows)]
            across = KAPPA * (total[j, pl.ds(1, rows)] - add)
            after = jnp.where(lane_of == LANES - 1, pltpu.roll(total[j + 1, pl.ds(0, rows)], LANES - 1, 1),
                              pltpu.roll(add, LANES - 1, 1))
            along = KAPPA * (after - add)
            for r in range(row_tiles):
                cut = slice(r * SUB, r * SUB + SUB)
                done[0, r, j] = final[cut]
                done[1, r, j] = across[cut]
                done[2, r, j] = along[cut]

    out_a = pltpu.make_async_copy(done, out_state, out_sem.at[0])
    out_a.start()

    for i in range(block):
        for r in range(row_tiles):
            gsum[r, i] = part[me * block + i, pl.ds(r * SUB, SUB)]

    @pl.loop(1, n)
    def _(d):
        source = lax.rem(me + n - d, n)
        pltpu.make_async_remote_copy(
            src_ref=part.at[pl.ds(0, block)], dst_ref=share.at[source],
            send_sem=rs_send.at[d], recv_sem=rs_recv.at[source],
            device_id={"path": source}, device_id_type=MESH).wait_recv()
        for i in range(block):
            for r in range(row_tiles):
                gsum[r, i] = gsum[r, i] + share[source, i, pl.ds(r * SUB, SUB)]

    out_b = pltpu.make_async_copy(gsum, out_grad, out_sem.at[1])
    out_b.start()

    for copy in sends:
        copy.wait_send()

    @pl.loop(1, n)
    def _(d):
        grad_copy(lax.rem(me + d, n), d).wait_send()

    @pl.when(has_up)
    def _():
        state_copy(0).wait_send()

        @pl.loop(0, n)
        def _(b):
            heat_copy(0, b).wait_send()

    @pl.when(has_down)
    def _():
        state_copy(1).wait_send()

        @pl.loop(0, n)
        def _(b):
            heat_copy(1, b).wait_send()

    out_a.wait()
    out_b.wait()


def tiled(x):
    lead, (rows, cols) = x.shape[:-2], x.shape[-2:]
    return jnp.swapaxes(x.reshape(*lead, rows // SUB, SUB, cols // LANES, LANES), -3, -2)


def untiled(x):
    lead, (row_tiles, cols) = x.shape[:-4], x.shape[-4:-2]
    return jnp.swapaxes(x, -3, -2).reshape(*lead, row_tiles * SUB, cols * LANES)


def per_device(n, tiles, state0, intensity, absorption, screen_adjoint):
    rows, columns = intensity.shape[1:]
    cols, row_tiles = columns // LANES, rows // SUB
    block = cols // n
    height = rows + 4 * SUB
    f32 = jnp.float32
    dma = pltpu.SemaphoreType.DMA
    state_adjoint, grad = pl.pallas_call(
        functools.partial(kernel, n, tiles),
        out_shape=(
            jax.ShapeDtypeStruct((3, row_tiles, cols, SUB, LANES), f32),
            jax.ShapeDtypeStruct((row_tiles, block, SUB, LANES), f32),
        ),
        in_specs=[pl.BlockSpec(memory_space=pl.ANY)] * 4,
        out_specs=[pl.BlockSpec(memory_space=pl.ANY)] * 2,
        scratch_shapes=[
            pltpu.VMEM((STEPS + 1, cols + 2, height, LANES), f32),
            pltpu.VMEM((STEPS + 1, cols + 2, height, LANES), f32),
            pltpu.VMEM((cols, rows + 2 * SUB, LANES), f32),
            pltpu.VMEM((2, cols, rows, LANES), f32),
            pltpu.VMEM((cols, rows, LANES), f32),
            pltpu.VMEM((cols, rows, LANES), f32),
            pltpu.VMEM((cols + 1, rows, LANES), f32),
            pltpu.VMEM((2, 2, cols, SUB, LANES), f32),
            pltpu.VMEM((cols + 1, rows + SUB, LANES), f32),
            pltpu.VMEM((cols, rows, LANES), f32),
            pltpu.VMEM((n, block, rows, LANES), f32),
            pltpu.VMEM((3, row_tiles, cols, SUB, LANES), f32),
            pltpu.VMEM((row_tiles, block, SUB, LANES), f32),
            dma((6 * row_tiles,)),
            dma((2 * n,)),
            dma((n,)),
            dma((2,)),
            dma((2,)),
            dma((2, n)),
            dma((2, n)),
            dma((n,)),
            dma((n,)),
            dma((2,)),
        ],
        compiler_params=pltpu.CompilerParams(
            collective_id=0, has_side_effects=True, vmem_limit_bytes=60 * 1024 * 1024),
    )(tiled(state0[:, 0]), tiled(intensity[0]), tiled(absorption), tiled(screen_adjoint))
    return (untiled(state_adjoint)[:, None], untiled(grad))


def solution(mesh):
    return jax.shard_map(
        functools.partial(per_device, mesh.shape["path"], mesh.shape["tile"]),
        mesh=mesh,
        in_specs=(
            P(None, "path", "tile", None),
            P("path", "tile", None),
            P("tile", "path"),
            P("tile", "path"),
        ),
        out_specs=(P(None, "path", "tile", None), P("tile", "path")),
        check_vma=False,
    )
```

```python
import functools

import jax
import jax.numpy as jnp
from jax import lax
from jax.experimental import pallas as pl
from jax.experimental.pallas import tpu as pltpu
from jax.sharding import PartitionSpec as P

MESH = pl.DeviceIdType.MESH
STEPS = 8
KAPPA = 0.65
DAMPING = 0.99
HEATING = 0.06
COUPLING = 0.5
LANES = 128
SUB = 8
DEPTH = 4
TOP = 2 * SUB
GROUP = 32
UNROLL = 8


def kernel(n, tiles, state, light, absorb, screen, out_state, out_grad,
           xb, yb, wy, maps, beam, ub, vb, stage, total, part, share, done, gsum,
           load_sem, ag_send, ag_recv, hx_send, hx_recv, hq_send, hq_recv, rs_send, rs_recv, out_sem):
    depth = DEPTH if n % DEPTH == 0 else 1
    wide = n // depth
    row_tiles, cols = light.shape[0], light.shape[1]
    rows = row_tiles * SUB
    span = rows + 2 * SUB
    block = cols // n
    group = GROUP if cols % GROUP == 0 else block
    me = lax.axis_index("path")
    tile = lax.axis_index("tile")
    my_z, my_y = me // wide, lax.rem(me, wide)
    has_up, has_down = tile > 0, tile < tiles - 1

    loads = []
    for i in range(row_tiles):
        low = pl.ds(i * SUB, SUB)
        own = pl.ds(me * block, block)
        for src, dst in (
            (absorb.at[i], maps.at[0, own, low]),
            (screen.at[i], maps.at[1, own, low]),
            (light.at[i], beam.at[:, low]),
            (state.at[1, i], ub.at[:, low]),
            (state.at[2, i], vb.at[pl.ds(1, cols), low]),
            (state.at[0, i], xb.at[1, pl.ds(1, cols), pl.ds(TOP + i * SUB, SUB)]),
        ):
            loads.append(pltpu.make_async_copy(src, dst, load_sem.at[len(loads)]))
            loads[-1].start()

    barrier = pltpu.get_barrier_semaphore()
    for d in range(1, n):
        pl.semaphore_signal(barrier, inc=1, device_id={"path": lax.rem(me + d, n)}, device_id_type=MESH)

    @pl.when(has_up)
    def _():
        pl.semaphore_signal(barrier, inc=1, device_id={"tile": tile - 1}, device_id_type=MESH)

    @pl.when(has_down)
    def _():
        pl.semaphore_signal(barrier, inc=1, device_id={"tile": tile + 1}, device_id_type=MESH)

    greeted = n - 1 + has_up.astype(jnp.int32) + has_down.astype(jnp.int32)
    pl.semaphore_wait(barrier, greeted)

    def map_copy(owner, target, slot):
        ref = maps.at[:, pl.ds(owner * block, block)]
        return pltpu.make_async_remote_copy(
            src_ref=ref, dst_ref=ref, send_sem=ag_send.at[slot], recv_sem=ag_recv.at[owner],
            device_id={"path": target}, device_id_type=MESH)

    for i in range(row_tiles):
        loads[6 * i].wait()
        loads[6 * i + 1].wait()
    sends = []
    for d in [x for x in (2, 1, 3) if x < depth]:
        sends.append(map_copy(me, lax.rem(my_z + d, depth) * wide + my_y, len(sends)))
        sends[-1].start()
    for d in range(1, wide):
        sends.append(map_copy(me, my_z * wide + lax.rem(my_y + d, wide), len(sends)))
        sends[-1].start()

    blank = jnp.zeros((span, LANES), jnp.float32)
    vb[0] = jnp.zeros((rows, LANES), jnp.float32)
    total[cols] = jnp.zeros((rows + SUB, LANES), jnp.float32)
    for t in range(1, STEPS + 1):
        xb[t, cols + 1, pl.ds(SUB, span)] = blank
        yb[t, cols + 1, pl.ds(SUB, span)] = blank

    @pl.loop(0, cols, unroll=UNROLL)
    def _(j):
        wy[j] = blank

    strip = jnp.zeros((2, SUB, LANES), jnp.float32)

    @pl.when(jnp.logical_not(has_up))
    def _():
        @pl.loop(0, cols, unroll=UNROLL)
        def _(j):
            xb[pl.ds(0, 2), 1 + j, pl.ds(SUB, SUB)] = strip
            yb[pl.ds(0, 2), 1 + j, pl.ds(SUB, SUB)] = strip

    @pl.when(jnp.logical_not(has_down))
    def _():
        @pl.loop(0, cols, unroll=UNROLL)
        def _(j):
            xb[pl.ds(0, 2), 1 + j, pl.ds(TOP + rows, SUB)] = strip
            yb[pl.ds(0, 2), 1 + j, pl.ds(TOP + rows, SUB)] = strip

    for i in range(row_tiles):
        for c in range(2, 6):
            loads[6 * i + c].wait()
    row_of = lax.broadcasted_iota(jnp.int32, (rows, LANES), 0)
    lane_of = lax.broadcasted_iota(jnp.int32, (rows, LANES), 1)

    @pl.loop(0, cols, unroll=UNROLL)
    def _(j):
        u, v = ub[j], vb[1 + j]
        before = jnp.where(row_of == 0, 0.0, pltpu.roll(u, 1, 0))
        left = jnp.where(lane_of == 0, pltpu.roll(vb[j], 1, 1), pltpu.roll(v, 1, 1))
        w = KAPPA * ((u - before) + (v - left))
        xb[0, 1 + j, pl.ds(TOP, rows)] = w
        density = xb[1, 1 + j, pl.ds(TOP, rows)]
        stage[0, 0, j] = w[:SUB]
        stage[0, 1, j] = density[:SUB]
        last = KAPPA * pltpu.roll(u[rows - SUB:], 1, 0)
        stage[1, 0, j] = jnp.where(row_of[:SUB] == 0, last, w[rows - SUB:])
        stage[1, 1, j] = density[rows - SUB:]

    def state_copy(way):
        return pltpu.make_async_remote_copy(
            src_ref=stage.at[way],
            dst_ref=xb.at[pl.ds(0, 2), pl.ds(1, cols), pl.ds(TOP + rows if way == 0 else SUB, SUB)],
            send_sem=hx_send.at[way], recv_sem=hx_recv.at[way],
            device_id={"tile": tile - 1 if way == 0 else tile + 1}, device_id_type=MESH)

    def heat_copy(way, owner):
        at = pl.ds(1 + owner * block, block)
        first = TOP if way == 0 else TOP + rows - SUB
        return pltpu.make_async_remote_copy(
            src_ref=yb.at[pl.ds(0, 2), at, pl.ds(first, SUB)],
            dst_ref=yb.at[pl.ds(0, 2), at, pl.ds(TOP + rows if way == 0 else SUB, SUB)],
            send_sem=hq_send.at[way, owner], recv_sem=hq_recv.at[way, owner],
            device_id={"tile": tile - 1 if way == 0 else tile + 1}, device_id_type=MESH)

    @pl.when(has_up)
    def _():
        state_copy(0).start()

    @pl.when(has_down)
    def _():
        state_copy(1).start()

    def use(owner):
        for i in range(block):
            j = owner * block + i
            yb[0, 1 + j, pl.ds(TOP, rows)] = HEATING * (maps[0, j] * beam[j])
            yb[1, 1 + j, pl.ds(TOP, rows)] = maps[1, j]

        @pl.when(has_up)
        def _():
            heat_copy(0, owner).start()

        @pl.when(has_down)
        def _():
            heat_copy(1, owner).start()

    use(me)
    for d in [x for x in (1, 3, 2) if x < depth]:
        owner = lax.rem(my_z + d, depth) * wide + my_y
        map_copy(owner, owner, 0).wait_recv()
        for e in range(1, wide):
            sends.append(map_copy(owner, my_z * wide + lax.rem(my_y + e, wide), len(sends)))
            sends[-1].start()
        use(owner)
    for d in [x for x in (0, 1, 3, 2) if x < depth]:
        for e in range(1, wide):
            owner = lax.rem(my_z + d, depth) * wide + lax.rem(my_y + e, wide)
            map_copy(owner, owner, 0).wait_recv()
            use(owner)

    @pl.when(has_up)
    def _():
        state_copy(1).wait_recv()

        @pl.loop(0, cols, unroll=UNROLL)
        def _(j):
            above = jnp.where(row_of[:SUB] == 0, xb[0, 1 + j, pl.ds(SUB, SUB)], 0.0)
            xb[0, 1 + j, pl.ds(TOP, SUB)] = xb[0, 1 + j, pl.ds(TOP, SUB)] - above

    @pl.when(has_down)
    def _():
        state_copy(0).wait_recv()

        @pl.loop(0, cols, unroll=UNROLL)
        def _(j):
            last = KAPPA * pltpu.roll(ub[j, pl.ds(rows - SUB, SUB)], 1, 0)
            above = jnp.where(row_of[:SUB] == 0, last, 0.0)
            xb[0, 1 + j, pl.ds(TOP + rows, SUB)] = xb[0, 1 + j, pl.ds(TOP + rows, SUB)] - above

    @pl.when(has_up)
    def _():
        @pl.loop(0, n)
        def _(b):
            heat_copy(1, b).wait_recv()

    @pl.when(has_down)
    def _():
        @pl.loop(0, n)
        def _(b):
            heat_copy(0, b).wait_recv()

    place = tile * rows - SUB + lax.broadcasted_iota(jnp.int32, (span, LANES), 0)
    inside = (place >= 0) & (place < tiles * rows)
    near = jnp.where(inside, KAPPA * KAPPA, 0.0)
    here = jnp.where(place == 0, 3.0, 4.0) * (KAPPA * KAPPA)
    lane = lax.broadcasted_iota(jnp.int32, (span, LANES), 1)

    def pad_left(field, t):
        field[t, 0, pl.ds(SUB, span)] = pltpu.roll(field[t, 1, pl.ds(SUB, span)], LANES - 1, 1)

    pad_left(xb, 1)
    pad_left(yb, 1)

    def spread(field, t, first, count, start, size, near, here, lane):
        window = [field[t, first + i, pl.ds(start, size)] for i in range(count + 2)]
        right = [pltpu.roll(x, 1, 1) for x in window[:-1]]
        left = [pltpu.roll(x, LANES - 1, 1) for x in window[1:]]
        found = []
        for i in range(count):
            before = jnp.where(lane == 0, right[i], right[i + 1])
            after = jnp.where(lane == LANES - 1, left[i + 1], left[i])
            upper = field[t, first + 1 + i, pl.ds(start - 1, size)]
            lower = field[t, first + 1 + i, pl.ds(start + 1, size)]
            x = window[i + 1]
            found.append((x, near * ((before + after) + (upper + lower)) - here * x))
        return found

    @pl.loop(1, STEPS)
    def _(t):
        @pl.loop(0, cols // group)
        def _(g):
            base = g * group
            args = (t, base, group, SUB, span, near, here, lane)
            for i, (x, change) in enumerate(spread(xb, *args)):
                heat = yb[0, base + 1 + i, pl.ds(SUB, span)]
                w = xb[0, base + 1 + i, pl.ds(SUB, span)] - change
                xb[0, base + 1 + i, pl.ds(SUB, span)] = w
                xb[t + 1, base + 1 + i, pl.ds(SUB, span)] = (DAMPING + COUPLING * heat) * x + (heat - w)
            for i, (y, change) in enumerate(spread(yb, *args)):
                heat = yb[0, base + 1 + i, pl.ds(SUB, span)]
                w = wy[base + i] - change
                wy[base + i] = w
                yb[t + 1, base + 1 + i, pl.ds(SUB, span)] = (DAMPING + COUPLING * heat) * y - w

        pad_left(xb, t + 1)
        pad_left(yb, t + 1)

    def grad_copy(owner, slot):
        return pltpu.make_async_remote_copy(
            src_ref=part.at[pl.ds(owner * block, block)], dst_ref=share.at[me],
            send_sem=rs_send.at[slot], recv_sem=rs_recv.at[me],
            device_id={"path": owner}, device_id_type=MESH)

    def gradient(owner):
        @pl.loop(0, block, unroll=block)
        def _(i):
            j = owner * block + i
            both = [yb[1 + t, 1 + j, pl.ds(TOP, rows + SUB)] for t in range(STEPS)]
            add = both[0]
            for t in range(1, STEPS):
                add = add + both[t]
            mix = both[STEPS - 1][:rows] * xb[1, 1 + j, pl.ds(TOP, rows)]
            for t in range(1, STEPS):
                mix = mix + both[STEPS - 1 - t][:rows] * xb[1 + t, 1 + j, pl.ds(TOP, rows)]
            total[j] = add
            part[j] = beam[j] * (HEATING * add[:rows] + (HEATING * COUPLING) * mix)

    @pl.loop(1, n)
    def _(d):
        owner = lax.rem(me + d, n)
        gradient(owner)
        grad_copy(owner, d).start()

    gradient(me)

    inner = slice(SUB, SUB + rows)

    @pl.loop(0, cols // group)
    def _(g):
        base = g * group
        found = spread(yb, STEPS, base, group, TOP, rows, near[inner], here[inner], lane[inner])
        for i, (y, change) in enumerate(found):
            j = base + i
            heat = yb[0, 1 + j, pl.ds(TOP, rows)]
            w = wy[j, pl.ds(SUB, rows)] - change
            final = (DAMPING + COUPLING * heat) * y - w
            add = total[j, pl.ds(0, rows)]
            across = KAPPA * (total[j, pl.ds(1, rows)] - add)
            after = jnp.where(lane_of == LANES - 1, pltpu.roll(total[j + 1, pl.ds(0, rows)], LANES - 1, 1),
                              pltpu.roll(add, LANES - 1, 1))
            along = KAPPA * (after - add)
            for r in range(row_tiles):
                cut = slice(r * SUB, r * SUB + SUB)
                done[0, r, j] = final[cut]
                done[1, r, j] = across[cut]
                done[2, r, j] = along[cut]

    out_a = pltpu.make_async_copy(done, out_state, out_sem.at[0])
    out_a.start()

    for i in range(block):
        for r in range(row_tiles):
            gsum[r, i] = part[me * block + i, pl.ds(r * SUB, SUB)]

    @pl.loop(1, n)
    def _(d):
        source = lax.rem(me + n - d, n)
        pltpu.make_async_remote_copy(
            src_ref=part.at[pl.ds(0, block)], dst_ref=share.at[source],
            send_sem=rs_send.at[d], recv_sem=rs_recv.at[source],
            device_id={"path": source}, device_id_type=MESH).wait_recv()
        for i in range(block):
            for r in range(row_tiles):
                gsum[r, i] = gsum[r, i] + share[source, i, pl.ds(r * SUB, SUB)]

    out_b = pltpu.make_async_copy(gsum, out_grad, out_sem.at[1])
    out_b.start()

    for copy in sends:
        copy.wait_send()

    @pl.loop(1, n)
    def _(d):
        grad_copy(lax.rem(me + d, n), d).wait_send()

    @pl.when(has_up)
    def _():
        state_copy(0).wait_send()

        @pl.loop(0, n)
        def _(b):
            heat_copy(0, b).wait_send()

    @pl.when(has_down)
    def _():
        state_copy(1).wait_send()

        @pl.loop(0, n)
        def _(b):
            heat_copy(1, b).wait_send()

    out_a.wait()
    out_b.wait()


def settle(state, grad, out_state, out_grad, state_held, grad_held, sem):
    pairs = [(state.at[c], state_held.at[c], out_state.at[c]) for c in range(3)] + [(grad, grad_held, out_grad)]
    gets = [pltpu.make_async_copy(x, y, sem.at[0, i]) for i, (x, y, z) in enumerate(pairs)]
    puts = [pltpu.make_async_copy(y, z, sem.at[1, i]) for i, (x, y, z) in enumerate(pairs)]
    for get in gets:
        get.start()
    for get, put in zip(gets, puts):
        get.wait()
        put.start()
    for put in puts:
        put.wait()


def tiled(x):
    lead, (rows, cols) = x.shape[:-2], x.shape[-2:]
    return jnp.swapaxes(x.reshape(*lead, rows // SUB, SUB, cols // LANES, LANES), -3, -2)


def untiled(x):
    lead, (row_tiles, cols) = x.shape[:-4], x.shape[-4:-2]
    return jnp.swapaxes(x, -3, -2).reshape(*lead, row_tiles * SUB, cols * LANES)


def per_device(n, tiles, state0, intensity, absorption, screen_adjoint):
    rows, columns = intensity.shape[1:]
    cols, row_tiles = columns // LANES, rows // SUB
    block = cols // n
    height = rows + 4 * SUB
    f32 = jnp.float32
    dma = pltpu.SemaphoreType.DMA
    shapes = (
        jax.ShapeDtypeStruct((3, row_tiles, cols, SUB, LANES), f32),
        jax.ShapeDtypeStruct((row_tiles, block, SUB, LANES), f32),
    )
    whole = pl.BlockSpec(memory_space=pl.ANY)
    found = pl.pallas_call(
        functools.partial(kernel, n, tiles),
        out_shape=shapes,
        in_specs=[whole] * 4,
        out_specs=[whole] * 2,
        scratch_shapes=[
            pltpu.VMEM((STEPS + 1, cols + 2, height, LANES), f32),
            pltpu.VMEM((STEPS + 1, cols + 2, height, LANES), f32),
            pltpu.VMEM((cols, rows + 2 * SUB, LANES), f32),
            pltpu.VMEM((2, cols, rows, LANES), f32),
            pltpu.VMEM((cols, rows, LANES), f32),
            pltpu.VMEM((cols, rows, LANES), f32),
            pltpu.VMEM((cols + 1, rows, LANES), f32),
            pltpu.VMEM((2, 2, cols, SUB, LANES), f32),
            pltpu.VMEM((cols + 1, rows + SUB, LANES), f32),
            pltpu.VMEM((cols, rows, LANES), f32),
            pltpu.VMEM((n, block, rows, LANES), f32),
            pltpu.VMEM((3, row_tiles, cols, SUB, LANES), f32),
            pltpu.VMEM((row_tiles, block, SUB, LANES), f32),
            dma((6 * row_tiles,)),
            dma((2 * n,)),
            dma((n,)),
            dma((2,)),
            dma((2,)),
            dma((2, n)),
            dma((2, n)),
            dma((n,)),
            dma((n,)),
            dma((2,)),
        ],
        compiler_params=pltpu.CompilerParams(
            collective_id=0, has_side_effects=True, vmem_limit_bytes=60 * 1024 * 1024),
    )(tiled(state0[:, 0]), tiled(intensity[0]), tiled(absorption), tiled(screen_adjoint))
    state_adjoint, grad = pl.pallas_call(
        settle,
        out_shape=shapes,
        in_specs=[whole] * 2,
        out_specs=[whole] * 2,
        scratch_shapes=[pltpu.VMEM(x.shape, f32) for x in shapes] + [dma((2, 4))],
        compiler_params=pltpu.CompilerParams(vmem_limit_bytes=60 * 1024 * 1024),
    )(*found)
    return (untiled(state_adjoint)[:, None], untiled(grad))


def solution(mesh):
    return jax.shard_map(
        functools.partial(per_device, mesh.shape["path"], mesh.shape["tile"]),
        mesh=mesh,
        in_specs=(
            P(None, "path", "tile", None),
            P("path", "tile", None),
            P("tile", "path"),
            P("tile", "path"),
        ),
        out_specs=(P(None, "path", "tile", None), P("tile", "path")),
        check_vma=False,
    )
```

```python
import functools

import jax
import jax.numpy as jnp
from jax import lax
from jax.experimental import pallas as pl
from jax.experimental.pallas import tpu as pltpu
from jax.sharding import PartitionSpec as P

MESH = pl.DeviceIdType.MESH
STEPS = 8
KAPPA = 0.65
DAMPING = 0.99
HEATING = 0.06
COUPLING = 0.5
LANES = 128
SUB = 8
DEPTH = 4
TOP = 2 * SUB
GROUP = 32
UNROLL = 8


def kernel(n, tiles, state, light, absorb, screen, out_state, out_grad,
           xb, yb, wy, maps, beam, ub, vb, stage, total, part, share, done, gsum,
           load_sem, ag_send, ag_recv, hx_send, hx_recv, hq_send, hq_recv, rs_send, rs_recv, out_sem):
    depth = DEPTH if n % DEPTH == 0 else 1
    wide = n // depth
    row_tiles, cols = light.shape[0], light.shape[1]
    rows = row_tiles * SUB
    span = rows + 2 * SUB
    block = cols // n
    group = GROUP if cols % GROUP == 0 else block
    me = lax.axis_index("path")
    tile = lax.axis_index("tile")
    my_z, my_y = me // wide, lax.rem(me, wide)
    has_up, has_down = tile > 0, tile < tiles - 1

    loads = []
    for i in range(row_tiles):
        low = pl.ds(i * SUB, SUB)
        own = pl.ds(me * block, block)
        for src, dst in (
            (absorb.at[i], maps.at[0, own, low]),
            (screen.at[i], maps.at[1, own, low]),
            (light.at[i], beam.at[:, low]),
            (state.at[1, i], ub.at[:, low]),
            (state.at[2, i], vb.at[pl.ds(1, cols), low]),
            (state.at[0, i], xb.at[1, pl.ds(1, cols), pl.ds(TOP + i * SUB, SUB)]),
        ):
            loads.append(pltpu.make_async_copy(src, dst, load_sem.at[len(loads)]))
            loads[-1].start()

    barrier = pltpu.get_barrier_semaphore()
    for d in range(1, n):
        pl.semaphore_signal(barrier, inc=1, device_id={"path": lax.rem(me + d, n)}, device_id_type=MESH)

    @pl.when(has_up)
    def _():
        pl.semaphore_signal(barrier, inc=1, device_id={"tile": tile - 1}, device_id_type=MESH)

    @pl.when(has_down)
    def _():
        pl.semaphore_signal(barrier, inc=1, device_id={"tile": tile + 1}, device_id_type=MESH)

    greeted = n - 1 + has_up.astype(jnp.int32) + has_down.astype(jnp.int32)
    pl.semaphore_wait(barrier, greeted)

    def map_copy(owner, target, slot):
        ref = maps.at[:, pl.ds(owner * block, block)]
        return pltpu.make_async_remote_copy(
            src_ref=ref, dst_ref=ref, send_sem=ag_send.at[slot], recv_sem=ag_recv.at[owner],
            device_id={"path": target}, device_id_type=MESH)

    for i in range(row_tiles):
        loads[6 * i].wait()
        loads[6 * i + 1].wait()
    sends = []
    for d in [x for x in (1, 3, 2) if x < depth]:
        sends.append(map_copy(me, lax.rem(my_z + d, depth) * wide + my_y, len(sends)))
        sends[-1].start()
    for d in range(1, wide):
        sends.append(map_copy(me, my_z * wide + lax.rem(my_y + d, wide), len(sends)))
        sends[-1].start()

    blank = jnp.zeros((span, LANES), jnp.float32)
    vb[0] = jnp.zeros((rows, LANES), jnp.float32)
    total[cols] = jnp.zeros((rows + SUB, LANES), jnp.float32)
    for t in range(1, STEPS + 1):
        xb[t, cols + 1, pl.ds(SUB, span)] = blank
        yb[t, cols + 1, pl.ds(SUB, span)] = blank

    @pl.loop(0, cols, unroll=UNROLL)
    def _(j):
        wy[j] = blank

    strip = jnp.zeros((2, SUB, LANES), jnp.float32)

    @pl.when(jnp.logical_not(has_up))
    def _():
        @pl.loop(0, cols, unroll=UNROLL)
        def _(j):
            xb[pl.ds(0, 2), 1 + j, pl.ds(SUB, SUB)] = strip
            yb[pl.ds(0, 2), 1 + j, pl.ds(SUB, SUB)] = strip

    @pl.when(jnp.logical_not(has_down))
    def _():
        @pl.loop(0, cols, unroll=UNROLL)
        def _(j):
            xb[pl.ds(0, 2), 1 + j, pl.ds(TOP + rows, SUB)] = strip
            yb[pl.ds(0, 2), 1 + j, pl.ds(TOP + rows, SUB)] = strip

    for i in range(row_tiles):
        for c in range(2, 6):
            loads[6 * i + c].wait()
    row_of = lax.broadcasted_iota(jnp.int32, (rows, LANES), 0)
    lane_of = lax.broadcasted_iota(jnp.int32, (rows, LANES), 1)

    @pl.loop(0, cols, unroll=UNROLL)
    def _(j):
        u, v = ub[j], vb[1 + j]
        before = jnp.where(row_of == 0, 0.0, pltpu.roll(u, 1, 0))
        left = jnp.where(lane_of == 0, pltpu.roll(vb[j], 1, 1), pltpu.roll(v, 1, 1))
        w = KAPPA * ((u - before) + (v - left))
        xb[0, 1 + j, pl.ds(TOP, rows)] = w
        density = xb[1, 1 + j, pl.ds(TOP, rows)]
        stage[0, 0, j] = w[:SUB]
        stage[0, 1, j] = density[:SUB]
        last = KAPPA * pltpu.roll(u[rows - SUB:], 1, 0)
        stage[1, 0, j] = jnp.where(row_of[:SUB] == 0, last, w[rows - SUB:])
        stage[1, 1, j] = density[rows - SUB:]

    def state_copy(way):
        return pltpu.make_async_remote_copy(
            src_ref=stage.at[way],
            dst_ref=xb.at[pl.ds(0, 2), pl.ds(1, cols), pl.ds(TOP + rows if way == 0 else SUB, SUB)],
            send_sem=hx_send.at[way], recv_sem=hx_recv.at[way],
            device_id={"tile": tile - 1 if way == 0 else tile + 1}, device_id_type=MESH)

    def heat_copy(way, owner):
        at = pl.ds(1 + owner * block, block)
        first = TOP if way == 0 else TOP + rows - SUB
        return pltpu.make_async_remote_copy(
            src_ref=yb.at[pl.ds(0, 2), at, pl.ds(first, SUB)],
            dst_ref=yb.at[pl.ds(0, 2), at, pl.ds(TOP + rows if way == 0 else SUB, SUB)],
            send_sem=hq_send.at[way, owner], recv_sem=hq_recv.at[way, owner],
            device_id={"tile": tile - 1 if way == 0 else tile + 1}, device_id_type=MESH)

    @pl.when(has_up)
    def _():
        state_copy(0).start()

    @pl.when(has_down)
    def _():
        state_copy(1).start()

    def use(owner):
        for i in range(block):
            j = owner * block + i
            yb[0, 1 + j, pl.ds(TOP, rows)] = HEATING * (maps[0, j] * beam[j])
            yb[1, 1 + j, pl.ds(TOP, rows)] = maps[1, j]

        @pl.when(has_up)
        def _():
            heat_copy(0, owner).start()

        @pl.when(has_down)
        def _():
            heat_copy(1, owner).start()

    use(me)
    for d in [x for x in (1, 3, 2) if x < depth]:
        owner = lax.rem(my_z + d, depth) * wide + my_y
        map_copy(owner, owner, 0).wait_recv()
        for e in range(1, wide):
            sends.append(map_copy(owner, my_z * wide + lax.rem(my_y + e, wide), len(sends)))
            sends[-1].start()
        use(owner)
    for d in [x for x in (0, 1, 3, 2) if x < depth]:
        for e in range(1, wide):
            owner = lax.rem(my_z + d, depth) * wide + lax.rem(my_y + e, wide)
            map_copy(owner, owner, 0).wait_recv()
            use(owner)

    @pl.when(has_up)
    def _():
        state_copy(1).wait_recv()

        @pl.loop(0, cols, unroll=UNROLL)
        def _(j):
            above = jnp.where(row_of[:SUB] == 0, xb[0, 1 + j, pl.ds(SUB, SUB)], 0.0)
            xb[0, 1 + j, pl.ds(TOP, SUB)] = xb[0, 1 + j, pl.ds(TOP, SUB)] - above

    @pl.when(has_down)
    def _():
        state_copy(0).wait_recv()

        @pl.loop(0, cols, unroll=UNROLL)
        def _(j):
            last = KAPPA * pltpu.roll(ub[j, pl.ds(rows - SUB, SUB)], 1, 0)
            above = jnp.where(row_of[:SUB] == 0, last, 0.0)
            xb[0, 1 + j, pl.ds(TOP + rows, SUB)] = xb[0, 1 + j, pl.ds(TOP + rows, SUB)] - above

    @pl.when(has_up)
    def _():
        @pl.loop(0, n)
        def _(b):
            heat_copy(1, b).wait_recv()

    @pl.when(has_down)
    def _():
        @pl.loop(0, n)
        def _(b):
            heat_copy(0, b).wait_recv()

    place = tile * rows - SUB + lax.broadcasted_iota(jnp.int32, (span, LANES), 0)
    inside = (place >= 0) & (place < tiles * rows)
    near = jnp.where(inside, KAPPA * KAPPA, 0.0)
    here = jnp.where(place == 0, 3.0, 4.0) * (KAPPA * KAPPA)
    lane = lax.broadcasted_iota(jnp.int32, (span, LANES), 1)

    def pad_left(field, t):
        field[t, 0, pl.ds(SUB, span)] = pltpu.roll(field[t, 1, pl.ds(SUB, span)], LANES - 1, 1)

    pad_left(xb, 1)
    pad_left(yb, 1)

    def spread(field, t, first, count, start, size, near, here, lane):
        window = [field[t, first + i, pl.ds(start, size)] for i in range(count + 2)]
        right = [pltpu.roll(x, 1, 1) for x in window[:-1]]
        left = [pltpu.roll(x, LANES - 1, 1) for x in window[1:]]
        found = []
        for i in range(count):
            before = jnp.where(lane == 0, right[i], right[i + 1])
            after = jnp.where(lane == LANES - 1, left[i + 1], left[i])
            upper = field[t, first + 1 + i, pl.ds(start - 1, size)]
            lower = field[t, first + 1 + i, pl.ds(start + 1, size)]
            x = window[i + 1]
            found.append((x, near * ((before + after) + (upper + lower)) - here * x))
        return found

    @pl.loop(1, STEPS)
    def _(t):
        @pl.loop(0, cols // group)
        def _(g):
            base = g * group
            args = (t, base, group, SUB, span, near, here, lane)
            for i, (x, change) in enumerate(spread(xb, *args)):
                heat = yb[0, base + 1 + i, pl.ds(SUB, span)]
                w = xb[0, base + 1 + i, pl.ds(SUB, span)] - change
                xb[0, base + 1 + i, pl.ds(SUB, span)] = w
                xb[t + 1, base + 1 + i, pl.ds(SUB, span)] = (DAMPING + COUPLING * heat) * x + (heat - w)
            for i, (y, change) in enumerate(spread(yb, *args)):
                heat = yb[0, base + 1 + i, pl.ds(SUB, span)]
                w = wy[base + i] - change
                wy[base + i] = w
                yb[t + 1, base + 1 + i, pl.ds(SUB, span)] = (DAMPING + COUPLING * heat) * y - w

        pad_left(xb, t + 1)
        pad_left(yb, t + 1)

    def grad_copy(owner, slot):
        return pltpu.make_async_remote_copy(
            src_ref=part.at[pl.ds(owner * block, block)], dst_ref=share.at[me],
            send_sem=rs_send.at[slot], recv_sem=rs_recv.at[me],
            device_id={"path": owner}, device_id_type=MESH)

    def gradient(owner):
        @pl.loop(0, block, unroll=block)
        def _(i):
            j = owner * block + i
            both = [yb[1 + t, 1 + j, pl.ds(TOP, rows + SUB)] for t in range(STEPS)]
            add = both[0]
            for t in range(1, STEPS):
                add = add + both[t]
            mix = both[STEPS - 1][:rows] * xb[1, 1 + j, pl.ds(TOP, rows)]
            for t in range(1, STEPS):
                mix = mix + both[STEPS - 1 - t][:rows] * xb[1 + t, 1 + j, pl.ds(TOP, rows)]
            total[j] = add
            part[j] = beam[j] * (HEATING * add[:rows] + (HEATING * COUPLING) * mix)

    @pl.loop(1, n)
    def _(d):
        owner = lax.rem(me + d, n)
        gradient(owner)
        grad_copy(owner, d).start()

    gradient(me)

    inner = slice(SUB, SUB + rows)

    @pl.loop(0, cols // group)
    def _(g):
        base = g * group
        found = spread(yb, STEPS, base, group, TOP, rows, near[inner], here[inner], lane[inner])
        for i, (y, change) in enumerate(found):
            j = base + i
            heat = yb[0, 1 + j, pl.ds(TOP, rows)]
            w = wy[j, pl.ds(SUB, rows)] - change
            final = (DAMPING + COUPLING * heat) * y - w
            add = total[j, pl.ds(0, rows)]
            across = KAPPA * (total[j, pl.ds(1, rows)] - add)
            after = jnp.where(lane_of == LANES - 1, pltpu.roll(total[j + 1, pl.ds(0, rows)], LANES - 1, 1),
                              pltpu.roll(add, LANES - 1, 1))
            along = KAPPA * (after - add)
            for r in range(row_tiles):
                cut = slice(r * SUB, r * SUB + SUB)
                done[0, r, j] = final[cut]
                done[1, r, j] = across[cut]
                done[2, r, j] = along[cut]

    out_a = pltpu.make_async_copy(done, out_state, out_sem.at[0])
    out_a.start()

    for i in range(block):
        for r in range(row_tiles):
            gsum[r, i] = part[me * block + i, pl.ds(r * SUB, SUB)]

    @pl.loop(1, n)
    def _(d):
        source = lax.rem(me + n - d, n)
        pltpu.make_async_remote_copy(
            src_ref=part.at[pl.ds(0, block)], dst_ref=share.at[source],
            send_sem=rs_send.at[d], recv_sem=rs_recv.at[source],
            device_id={"path": source}, device_id_type=MESH).wait_recv()
        for i in range(block):
            for r in range(row_tiles):
                gsum[r, i] = gsum[r, i] + share[source, i, pl.ds(r * SUB, SUB)]

    out_b = pltpu.make_async_copy(gsum, out_grad, out_sem.at[1])
    out_b.start()

    for copy in sends:
        copy.wait_send()

    @pl.loop(1, n)
    def _(d):
        grad_copy(lax.rem(me + d, n), d).wait_send()

    @pl.when(has_up)
    def _():
        state_copy(0).wait_send()

        @pl.loop(0, n)
        def _(b):
            heat_copy(0, b).wait_send()

    @pl.when(has_down)
    def _():
        state_copy(1).wait_send()

        @pl.loop(0, n)
        def _(b):
            heat_copy(1, b).wait_send()

    out_a.wait()
    out_b.wait()


def settle(state, grad, out_state, out_grad, state_held, grad_held, sem):
    pairs = [(state.at[c], state_held.at[c], out_state.at[c]) for c in range(3)] + [(grad, grad_held, out_grad)]
    gets = [pltpu.make_async_copy(x, y, sem.at[0, i]) for i, (x, y, z) in enumerate(pairs)]
    puts = [pltpu.make_async_copy(y, z, sem.at[1, i]) for i, (x, y, z) in enumerate(pairs)]
    for get in gets:
        get.start()
    for get, put in zip(gets, puts):
        get.wait()
        put.start()
    for put in puts:
        put.wait()


def tiled(x):
    lead, (rows, cols) = x.shape[:-2], x.shape[-2:]
    return jnp.swapaxes(x.reshape(*lead, rows // SUB, SUB, cols // LANES, LANES), -3, -2)


def untiled(x):
    lead, (row_tiles, cols) = x.shape[:-4], x.shape[-4:-2]
    return jnp.swapaxes(x, -3, -2).reshape(*lead, row_tiles * SUB, cols * LANES)


def per_device(n, tiles, state0, intensity, absorption, screen_adjoint):
    rows, columns = intensity.shape[1:]
    cols, row_tiles = columns // LANES, rows // SUB
    block = cols // n
    height = rows + 4 * SUB
    f32 = jnp.float32
    dma = pltpu.SemaphoreType.DMA
    shapes = (
        jax.ShapeDtypeStruct((3, row_tiles, cols, SUB, LANES), f32),
        jax.ShapeDtypeStruct((row_tiles, block, SUB, LANES), f32),
    )
    whole = pl.BlockSpec(memory_space=pl.ANY)
    found = pl.pallas_call(
        functools.partial(kernel, n, tiles),
        out_shape=shapes,
        in_specs=[whole] * 4,
        out_specs=[whole] * 2,
        scratch_shapes=[
            pltpu.VMEM((STEPS + 1, cols + 2, height, LANES), f32),
            pltpu.VMEM((STEPS + 1, cols + 2, height, LANES), f32),
            pltpu.VMEM((cols, rows + 2 * SUB, LANES), f32),
            pltpu.VMEM((2, cols, rows, LANES), f32),
            pltpu.VMEM((cols, rows, LANES), f32),
            pltpu.VMEM((cols, rows, LANES), f32),
            pltpu.VMEM((cols + 1, rows, LANES), f32),
            pltpu.VMEM((2, 2, cols, SUB, LANES), f32),
            pltpu.VMEM((cols + 1, rows + SUB, LANES), f32),
            pltpu.VMEM((cols, rows, LANES), f32),
            pltpu.VMEM((n, block, rows, LANES), f32),
            pltpu.VMEM((3, row_tiles, cols, SUB, LANES), f32),
            pltpu.VMEM((row_tiles, block, SUB, LANES), f32),
            dma((6 * row_tiles,)),
            dma((2 * n,)),
            dma((n,)),
            dma((2,)),
            dma((2,)),
            dma((2, n)),
            dma((2, n)),
            dma((n,)),
            dma((n,)),
            dma((2,)),
        ],
        compiler_params=pltpu.CompilerParams(
            collective_id=0, has_side_effects=True, vmem_limit_bytes=60 * 1024 * 1024),
    )(tiled(state0[:, 0]), tiled(intensity[0]), tiled(absorption), tiled(screen_adjoint))
    state_adjoint, grad = pl.pallas_call(
        settle,
        out_shape=shapes,
        in_specs=[whole] * 2,
        out_specs=[whole] * 2,
        scratch_shapes=[pltpu.VMEM(x.shape, f32) for x in shapes] + [dma((2, 4))],
        compiler_params=pltpu.CompilerParams(vmem_limit_bytes=60 * 1024 * 1024),
    )(*found)
    return (untiled(state_adjoint)[:, None], untiled(grad))


def solution(mesh):
    return jax.shard_map(
        functools.partial(per_device, mesh.shape["path"], mesh.shape["tile"]),
        mesh=mesh,
        in_specs=(
            P(None, "path", "tile", None),
            P("path", "tile", None),
            P("tile", "path"),
            P("tile", "path"),
        ),
        out_specs=(P(None, "path", "tile", None), P("tile", "path")),
        check_vma=False,
    )
```
